32 devices in a mesh: energy: 8 (over y, x, core), slab: 4 (over z).
Axes of the slice: x: 2, y: 2, z: 4, core: 2. Of those that a mesh axis runs over, the one named last changes fastest.
Arguments:
- left_green: bfloat16 [2, 8, 4, 512, 512], P(None, 'energy', 'slab'), may hold values from -0.1875 to 0.1875
- coupling: bfloat16 [4, 512, 512], P('slab'), may hold values from -0.1875 to 0.1875
- previous_lesser: bfloat16 [2, 8, 4, 512, 512], P(None, 'energy', 'slab'), may hold values from -3 to 3
- screened: bfloat16 [2, 4, 512, 512], P(None, 'slab'), may hold values from -6 to 6
- offsets: int32 [8, 2], P('energy'), may hold values from 1 to 3, as said below
- occupation: float32 [2], replicated, may hold values from 0.25 to 4
Outputs:
- lesser: bfloat16 [2, 8, 4, 512, 512], P(None, 'energy', 'slab')
The draws below stay inside these ranges and needn't reach their ends.
Inputs may be any that keep to these rules, and one draw needn't show every extreme that they name: `offsets`: every entry is a whole number of energy points from 1 to 3; both ends occur in every draw.
All inputs are finite; a program needn't handle non-finite values.
Results may differ from the reference program's by a relative error of at most 0.0075.
Values may be sent and summed in bfloat16 or wider, within the bound.
No kernel may reach another device: no remote copies, remote signals or barrier semaphores. Data moves between devices by JAX's collectives and lax.ppermute only.
A program may use at most 64 MiB of HBM per device.

```python
import math
import jax
import jax.numpy as jnp
from jax import lax

M = 512
MODES = 2
REACH = 3
ENERGIES = 8
SLABS = 4


def draw_offsets(key, part):
    key = jax.random.fold_in(key, 7)
    first, second = jax.random.split(key)
    values = jax.random.randint(first, (ENERGIES, MODES), 1, REACH + 1)
    spots = jax.random.randint(second, (2,), 0, ENERGIES)
    values = values.at[spots[0], 0].set(REACH)
    values = values.at[spots[1], 1].set(1)
    return values.astype(jnp.int32)


def block_levels(stream_key, shape, shards, least, largest):
    def one(position, parts):
        steps = jax.random.uniform(jax.random.fold_in(jax.random.fold_in(stream_key, 6), position), (parts,), jnp.float32, least / len(shards), largest / len(shards))
        return jnp.repeat(jnp.exp(steps), shape[position] // parts).reshape((-1,) + (1,) * (len(shape) - position - 1))

    factor_of = one(*shards[0])
    for cut in shards[1:]:
        factor_of = factor_of * one(*cut)
    return factor_of


def bell_draw(rng, shape, spread, limit, pieces=(), kind=jnp.bfloat16):
    entries = jax.random.normal(rng, shape, jnp.float32) * spread
    if len(pieces) > 0:
        entries = block_levels(rng, shape, pieces, -0.22, 0.18) * entries
    return jnp.clip(entries, min=-limit, max=limit).astype(kind)


def setup_inputs(seed: int = 0) -> dict:
    streams_of = jax.random.split(jax.random.key(seed), 7)
    left_green = bell_draw(streams_of[0], (2, ENERGIES, SLABS, M, M), (2 * M) ** -0.5, 0.1875, ((1, 8), (2, 4)))
    coupling = bell_draw(streams_of[1], (SLABS, M, M), (2 * M) ** -0.5, 0.1875, ((0, 4),))
    previous_lesser = bell_draw(streams_of[2], (2, ENERGIES, SLABS, M, M), 0.5, 3.0, ((1, 8), (2, 4)))
    screened = bell_draw(streams_of[3], (MODES, SLABS, M, M), 1.0, 6.0, ((1, 4),))
    offsets = draw_offsets(jax.random.fold_in(streams_of[6], 71), 0)
    occupation = jnp.clip(jnp.exp(jax.random.uniform(streams_of[5], (MODES,), jnp.float32, math.log(0.25), math.log(4.0))), 0.25, 4.0)
    return {"left_green": left_green, "coupling": coupling, "previous_lesser": previous_lesser, "screened": screened, "offsets": offsets, "occupation": occupation}


def matmul_plain(left, right):
    return jnp.dot(left.astype(jnp.float32), right.astype(jnp.float32), precision=lax.Precision.HIGHEST)


def matmul_trans(left, right):
    return lax.dot_general(left.astype(jnp.float32), right.astype(jnp.float32), (((1,), (1,)), ((), ())), precision=lax.Precision.HIGHEST)


def complex_times(left, right):
    real_part = matmul_plain(left[0], right[0]) - matmul_plain(left[1], right[1])
    imag_part = matmul_plain(left[0], right[1]) + matmul_plain(left[1], right[0])
    return jnp.stack([real_part, imag_part])


def complex_adjoint(left, right):
    real_part = matmul_trans(left[0], right[0]) + matmul_trans(left[1], right[1])
    imag_part = matmul_trans(left[1], right[0]) - matmul_trans(left[0], right[1])
    return jnp.stack([real_part, imag_part])


def complex_real(left, right):
    return jnp.stack([matmul_plain(left[0], right), matmul_plain(left[1], right)])


def reference(left_green, coupling, previous_lesser, screened, offsets, occupation):
    def one_energy(energy_id):
        green = lax.dynamic_index_in_dim(left_green, energy_id, 1, keepdims=False)
        self_energy = jnp.zeros((2, SLABS, M, M), jnp.float32)
        for mode in range(MODES):
            offset = offsets[energy_id, mode]
            higher = (energy_id + offset) % ENERGIES
            lower = (energy_id - offset + ENERGIES) % ENERGIES
            above = lax.dynamic_index_in_dim(previous_lesser, higher.astype(jnp.int32), 1, keepdims=False)
            below = lax.dynamic_index_in_dim(previous_lesser, lower.astype(jnp.int32), 1, keepdims=False)
            self_energy = self_energy + screened[mode].astype(jnp.float32)[None] * (above.astype(jnp.float32) + occupation[mode] * below.astype(jnp.float32))
        self_energy = self_energy.astype(jnp.bfloat16)

        def slab_step(state, inputs):
            green_slab, coupling_slab, self_slab = inputs
            transfer = complex_real(green_slab, coupling_slab).astype(jnp.bfloat16)
            half = complex_times(green_slab, self_slab).astype(jnp.bfloat16)
            source = complex_adjoint(half, green_slab).astype(jnp.bfloat16)
            carried = complex_times(transfer, state).astype(jnp.bfloat16)
            result = (complex_adjoint(carried, transfer) + source.astype(jnp.float32)).astype(jnp.bfloat16)
            return result, result

        start = jnp.zeros((2, M, M), jnp.bfloat16)
        inputs = (jnp.transpose(green, (1, 0, 2, 3)), coupling, jnp.transpose(self_energy, (1, 0, 2, 3)))
        final, results = lax.scan(slab_step, start, inputs)
        return jnp.transpose(results, (1, 0, 2, 3))

    stacked = lax.map(one_energy, jnp.arange(ENERGIES, dtype=jnp.int32))
    return jnp.transpose(stacked, (1, 0, 2, 3, 4))
```

```python
import functools

import jax
import jax.numpy as jnp
from jax import lax
from jax.experimental import pallas as pl
from jax.experimental.pallas import tpu as pltpu
from jax.sharding import PartitionSpec as P

MODES = 2
REACH = 3
BF = jnp.bfloat16
F32 = jnp.float32
CUTS = 2

VMEM = pl.BlockSpec(memory_space=pltpu.VMEM)
SMEM = pl.BlockSpec(memory_space=pltpu.SMEM)
ANY = pl.BlockSpec(memory_space=pl.ANY)


def dot(left, right):
    return jnp.dot(left, right, preferred_element_type=F32)


def dot_t(left, right):
    return lax.dot_general(left, right, (((1,), (1,)), ((), ())), preferred_element_type=F32)


def call(kernel, outs, scalars, arrays, flops, scratch=(), after=(), tied=()):
    moved = sum(a.size * a.dtype.itemsize for a in [*arrays, *outs])
    inputs, extra = len(scalars) + len(arrays), len(after) + len(tied)

    def body(*refs):
        rest = refs[inputs + extra :]
        kernel(*refs[:inputs], *rest[: len(outs)], *rest[len(outs) + len(tied) :])

    found = pl.pallas_call(
        body,
        out_shape=[*outs, *(jax.ShapeDtypeStruct(t.shape, t.dtype) for t in tied)],
        in_specs=[SMEM] * len(scalars) + [VMEM] * len(arrays) + [ANY] * extra,
        out_specs=[VMEM] * len(outs) + [ANY] * len(tied),
        scratch_shapes=list(scratch),
        input_output_aliases={
            inputs + len(after) + n: len(outs) + n for n in range(len(tied))
        },
        compiler_params=pltpu.CompilerParams(vmem_limit_bytes=24 * 2**20),
        cost_estimate=pl.CostEstimate(flops=flops, bytes_accessed=moved, transcendentals=0),
    )(*scalars, *arrays, *after, *tied)
    return found[0] if len(found) == 1 else found


def block(*shape):
    return jax.ShapeDtypeStruct(shape, BF)


def either(core_ref, number, work):
    for n in range(2):
        pl.when(core_ref[0] == (number ^ n))(functools.partial(work, n))


def self_energy_patch(spots, scalars, carriers, occupation, screened, pieces, results):
    rows, width = screened.shape[1:]

    def kernel(*refs):
        refs = list(refs)
        scalar_refs = [refs.pop(0) for _ in scalars]
        occ_ref = refs.pop(0)
        carrier_refs = [refs.pop(0) for _ in carriers]
        screened_ref = refs.pop(0)
        table = refs.pop()
        notes = [lambda ref=ref: ref[:, :128].astype(jnp.int32) for ref in carrier_refs]
        for n in range(len(pieces)):
            piece_ref = refs.pop(0)
            if len(piece_ref.shape) == 3:
                table[n] = piece_ref[...]
            else:
                table[n, 0] = piece_ref[:rows]
                table[n, 1] = piece_ref[rows : 2 * rows]
                notes.append(
                    lambda ref=piece_ref: ref[2 * rows : 2 * rows + 16, :128].astype(jnp.int32)
                )
        places = spots(scalar_refs, notes)
        step = 16

        def strip(i, carry):
            at = pl.ds(pl.multiple_of(i * step, step), step)
            weights = [screened_ref[m, at, :].astype(F32) for m in range(MODES)]
            for n in range(results):
                for part in range(2):
                    total = None
                    for m in range(MODES):
                        above = table[places[n][m][0], part, at, :].astype(F32)
                        below = table[places[n][m][1], part, at, :].astype(F32)
                        term = weights[m] * (above + occ_ref[m] * below)
                        total = term if total is None else total + term
                    refs[n][part, at, :] = total.astype(BF)
            return carry

        lax.fori_loop(0, rows // step, strip, 0)

    return call(
        kernel,
        [block(2, rows, width)] * results,
        [*scalars, occupation],
        [*carriers, screened, *pieces],
        results * 2 * rows * width * 12,
        [pltpu.VMEM((len(pieces), 2, rows, width), BF)],
    )


def times_into(left, right, out):
    size = left.shape[1]
    tile = min(256, size)
    real, imag = right[0], right[1]
    for i in range(0, size, tile):
        lr, li = left[0, i : i + tile, :], left[1, i : i + tile, :]
        out[0, i : i + tile, :] = (dot(lr, real) - dot(li, imag)).astype(BF)
        out[1, i : i + tile, :] = (dot(lr, imag) + dot(li, real)).astype(BF)


def times(core, number, lefts, groups, places=None, after=(), tied=()):
    rows, width = groups[0][0].shape[1:]
    full = (2, rows * len(groups), width)
    counts = [len(group) for group in groups]
    scalars = [core] if places is None else [core, places]
    whole = counts == [1]

    def kernel(core_ref, *refs):
        refs = list(refs)
        places_ref = refs.pop(0) if places is not None else None
        left_refs = [refs.pop(0) for _ in range(2)]
        if whole:
            right, out_ref = refs
        else:
            right, out_ref = refs.pop(), refs.pop()
            for n, count in enumerate(counts):
                if places_ref is None:
                    at = slice(n * rows, (n + 1) * rows)
                else:
                    at = pl.ds(pl.multiple_of(places_ref[n] * rows, rows), rows)
                value = refs.pop(0)[...]
                for _ in range(count - 1):
                    value = value + refs.pop(0)[...]
                right[:, at, :] = value
        either(core_ref, number, lambda n: times_into(left_refs[n], right, out_ref))

    return call(
        kernel,
        [block(*full)],
        scalars,
        [*lefts, *sum(groups, [])],
        8 * full[1] * full[1] * width,
        [] if whole else [pltpu.VMEM(full, BF)],
        after,
        tied,
    )


def transfer_of(green, coupling, after=()):
    size = coupling.shape[0]

    def kernel(green_ref, coupling_ref, out_ref):
        for part in range(2):
            out_ref[part] = dot(green_ref[part], coupling_ref[...]).astype(BF)

    return call(kernel, [block(*green.shape)], [], [green, coupling], 4 * size**3, (), after)


def composed(wanted, left, groups, after=()):
    size = left.shape[1]

    def kernel(wanted_ref, left_ref, *refs):
        *right_refs, out_ref, right = refs

        @pl.when(wanted_ref[0] == 1)
        def _():
            value = right_refs[0][...]
            for ref in right_refs[1:]:
                value = value + ref[...]
            right[...] = value
            times_into(left_ref, right, out_ref)

        @pl.when(wanted_ref[0] != 1)
        def _():
            out_ref[...] = left_ref[...]

    return call(
        kernel,
        [block(*left.shape)],
        [wanted],
        [left, *groups],
        8 * size**3,
        [pltpu.VMEM(left.shape, BF)],
        after,
    )


def adjoint_into(mine, theirs, right, mine_at, theirs_at, to_at, store):
    size = right.shape[1]
    tile = min(256, size)
    a = [right[p, to_at, mine_at] for p in range(2)]
    b = [right[p, to_at, theirs_at] for p in range(2)]
    for i in range(0, size, tile):
        at = slice(i, i + tile)
        mr, mi = mine[0, at, :], mine[1, at, :]
        tr, ti = theirs[0, at, :], theirs[1, at, :]
        real = dot_t(mr, a[0]) + dot_t(mi, a[1]) + dot_t(tr, b[0]) + dot_t(ti, b[1])
        imag = dot_t(mi, a[0]) - dot_t(mr, a[1]) + dot_t(ti, b[0]) - dot_t(tr, b[1])
        store(at, real, imag)


def adjoint_half(core, number, mine, theirs, rights, summand=None, after=()):
    half = mine.shape[2]

    def kernel(core_ref, mine_ref, theirs_ref, *refs):
        out_ref = refs[-1]

        def store(at, real, imag):
            if summand is not None:
                real = real + refs[2][0, at, :].astype(F32)
                imag = imag + refs[2][1, at, :].astype(F32)
            out_ref[0, at, :] = real.astype(BF)
            out_ref[1, at, :] = imag.astype(BF)

        def work(n):
            held = number ^ n
            own, other = slice(held * half, (held + 1) * half), slice((1 - held) * half, (2 - held) * half)
            adjoint_into(mine_ref, theirs_ref, refs[n], own, other, own, store)

        either(core_ref, number, work)

    arrays = [mine, theirs, *rights] + ([] if summand is None else [summand])
    flops = 16 * mine.shape[1] * half * half
    return call(kernel, [block(*mine.shape)], [core], arrays, flops, (), after)


def adjoint_own(core, mines, theirs, right, sums, other_sums):
    half = mines[0].shape[2]
    size = mines[0].shape[1]

    def kernel(core_ref, right_ref, *refs):
        out_ref = refs[-1]

        def work(n):
            mine_ref, theirs_ref, sum_ref, other_ref = refs[n:-1:2]
            own, other = slice(n * half, (n + 1) * half), slice((1 - n) * half, (2 - n) * half)
            for to, summand in ((own, sum_ref), (other, other_ref)):

                def store(at, real, imag):
                    out_ref[0, at, to] = (real + summand[0, at, :].astype(F32)).astype(BF)
                    out_ref[1, at, to] = (imag + summand[1, at, :].astype(F32)).astype(BF)

                adjoint_into(mine_ref, theirs_ref, right_ref, own, other, to, store)

        either(core_ref, 0, work)

    arrays = [right, *mines, *theirs, *sums, *other_sums]
    return call(kernel, [block(2, size, size)], [core], arrays, 8 * size**3)


def on_device(left_green, coupling, previous_lesser, screened, offsets, occupation):
    energies, slabs = lax.axis_size("energy"), lax.axis_size("slab")
    me, slab = lax.axis_index("energy"), lax.axis_index("slab")
    pairs = energies // 2
    pair, core = me // 2, me % 2
    first = core == 0
    size = coupling.shape[1]
    half = size // 2
    core_s = core[None]

    def swap(value):
        return lax.ppermute(value, "energy", [(i, i ^ 1) for i in range(energies)])

    def to_even(value):
        return lax.ppermute(value, "energy", [(i + 1, i) for i in range(0, energies, 2)])

    def to_odd(value):
        return lax.ppermute(value, "energy", [(i, i + 1) for i in range(0, energies, 2)])

    def by_energy(own, other):
        return jnp.where(first, own, other), jnp.where(first, other, own)

    green = left_green[:, 0, 0]
    before = previous_lesser[:, 0, 0]
    own = transfer_of(green, coupling[0])

    def column_half(value):
        return lax.dynamic_slice_in_dim(value, core * half, half, value.ndim - 1)

    both = [before, swap(before)]
    two = jnp.concatenate([offsets, swap(offsets)])
    spread = pairs in (2, 4) and size % (16 * pairs) == 0
    if spread:
        rows = size // pairs

        def across(value, d):
            moves = [(i, i ^ (2 * d)) for i in range(energies)]
            return lax.ppermute(value, "energy", moves)

        def patch(value, which):
            corner = (0, which * rows, core * half)
            return lax.dynamic_slice(value, corner, (2, rows, half))

        notes = jnp.pad(two.reshape(2 * MODES, 1).astype(BF), ((0, 16 - 2 * MODES), (0, 0)))
        notes = jnp.broadcast_to(notes, (16, half))
        order = list(reversed(range(1, pairs)))
        pieces = [None] * energies
        carriers = [notes]
        pieces[0], pieces[1] = patch(both[0], pair), patch(both[1], pair)
        for d in order:
            pieces[2 * d] = across(patch(both[0], pair ^ d), d)
        for d in order:
            sent = patch(both[1], pair ^ d).reshape(2 * rows, half)
            pieces[2 * d + 1] = across(jnp.concatenate([sent, notes]), d)
        weights = patch(screened[:, 0], pair)
        places = pair ^ jnp.arange(pairs, dtype=jnp.int32)
        scalars = [me[None]]

        def spots(scalar_refs, carrier_refs):
            here = scalar_refs[0][0]
            found = [[None] * pairs for _ in range(2)]
            core_here = lax.rem(here, 2)
            for d in range(pairs):
                note = carrier_refs[d]()
                line = lax.broadcasted_iota(jnp.int32, note.shape, 0)
                for n in range(2):
                    holder = here ^ (2 * d) ^ (core_here ^ n)
                    at = []
                    for m in range(MODES):
                        wanted_line = MODES * (core_here ^ n) + m
                        o = jnp.max(jnp.where(line == wanted_line, note, 0))
                        higher = lax.rem(holder + o, energies) ^ here
                        lower = lax.rem(holder - o + energies, energies) ^ here
                        at.append((higher, lower))
                    found[n][d] = at
            return found[0] + found[1]
    else:
        near = (REACH + 1) // 2
        pieces = []
        for d in range(-near, near + 1):
            moves = [(i, (i - 2 * d) % energies) for i in range(energies)]
            for value in both:
                value = column_half(value)
                pieces.append(lax.ppermute(value, "energy", moves) if d else value)
        weights = column_half(screened[:, 0])
        places, carriers = None, []
        scalars = [core_s, two]

        def spots(scalar_refs, piece_refs):
            core_ref, two_ref = scalar_refs

            def place(away):
                away = away + 2 * near
                return 2 * lax.div(away, 2) + (lax.rem(away, 2) ^ core_ref[0])

            found = []
            for n in range(2):
                shift = [two_ref[core_ref[0] ^ n, m] for m in range(MODES)]
                found.append([(place(n + o), place(n - o)) for o in shift])
            return found

    def maps_before(span, own):
        found, moving = [], own
        for hop in range(span):
            moves = [
                (s + hop - 1, s + hop)
                for s in range(3 * span, slabs, 2 * span)
                if s + hop < slabs
            ]
            moving = lax.ppermute(moving, "slab", moves)
            found.append(moving)
        return found

    befores = maps_before(1, own) if slabs > 2 else []
    other_green = swap(green)
    lefts = (green, other_green)
    found = self_energy_patch(
        spots, scalars, carriers, occupation, weights, pieces, 2 * pairs if spread else 2
    )
    sums = []
    if spread:
        early, late = list(found[:pairs]), list(found[pairs:])
        for d in order:
            early[d] = across(early[d], d)
        product, *late[1:] = times(
            core_s, 0, lefts, [[part] for part in early], places, tied=late[1:]
        )
        for d in order:
            late[d] = across(late[d], d)
    else:
        product = times(core_s, 0, lefts, [[found[0]]])
        late = [found[1]]
    sums.append(adjoint_half(core_s, 0, product, swap(product), lefts, None, befores))
    product = times(core_s, 1, lefts, [[part] for part in late], places, after=sums)
    sums.append(adjoint_half(core_s, 1, product, swap(product), lefts))
    maps = (own, transfer_of(other_green, coupling[0], after=sums[1:]))

    def arrivals(span, value):
        cuts = 1 if span == 1 else CUTS
        high = size // cuts
        groups = []
        for cut in range(cuts):
            group, moving = [], value[:, cut * high : (cut + 1) * high]
            for hop in range(span):
                moves = [
                    (s + hop - 1, s + hop)
                    for s in range(span, slabs, 2 * span)
                    if s + hop < slabs
                ]
                moving = lax.ppermute(moving, "slab", moves)
                group.append(moving)
            groups.append(group)
        return groups

    span = 1
    groups = [arrivals(1, value) for value in sums] if slabs > 1 else []
    while 2 * span < slabs:
        wanted = lax.rem(slab // span, 2)[None]
        own = composed(wanted, own, befores, after=[sums[1], maps[1]])
        carried = times(core_s, 0, maps, groups[0], after=[own])
        early = adjoint_half(core_s, 0, carried, swap(carried), maps, sums[0])
        early_groups = arrivals(2 * span, early)
        heads = [group[0] for group in early_groups]
        carried = times(core_s, 1, maps, groups[1], after=[early, heads[0]])
        behind = heads[1:] + early_groups[0][1:2]
        late = adjoint_half(core_s, 1, carried, swap(carried), maps, sums[1], behind)
        sums, groups = [early, late], [early_groups, arrivals(2 * span, late)]
        maps = (own, swap(own))
        span *= 2
        if 2 * span < slabs:
            befores = maps_before(span, own)
    if slabs > 1:
        carried = [times(core_s, n, maps, groups[n]) for n in range(2)]
        theirs = [to_even(carried[0]), to_odd(carried[1])]
        others = [to_even(sums[0]), to_odd(sums[1])]
        result = adjoint_own(core_s, carried, theirs, maps[0], sums, others)
        return result[:, None, None]
    result = jnp.where(first, sums[0], sums[1])
    other = swap(jnp.where(first, sums[1], sums[0]))
    return jnp.concatenate(by_energy(result, other), axis=2)[:, None, None]


def solution(mesh):
    placed = (
        P(None, "energy", "slab", None, None),
        P("slab", None, None),
        P(None, "energy", "slab", None, None),
        P(None, "slab", None, None),
        P("energy", None),
        P(),
    )
    return jax.shard_map(
        on_device,
        mesh=mesh,
        in_specs=placed,
        out_specs=P(None, "energy", "slab", None, None),
        check_vma=False,
    )
```

```python
import functools

import jax
import jax.numpy as jnp
from jax import lax
from jax.experimental import pallas as pl
from jax.experimental.pallas import tpu as pltpu
from jax.sharding import PartitionSpec as P

MODES = 2
REACH = 3
BF = jnp.bfloat16
F32 = jnp.float32
CUTS = 2
PARTS = 1
AHEAD = 0

VMEM = pl.BlockSpec(memory_space=pltpu.VMEM)
SMEM = pl.BlockSpec(memory_space=pltpu.SMEM)
ANY = pl.BlockSpec(memory_space=pl.ANY)


def dot(left, right):
    return jnp.dot(left, right, preferred_element_type=F32)


def dot_t(left, right):
    return lax.dot_general(left, right, (((1,), (1,)), ((), ())), preferred_element_type=F32)


def call(kernel, outs, scalars, arrays, flops, scratch=(), after=(), tied=()):
    moved = sum(a.size * a.dtype.itemsize for a in [*arrays, *outs])
    inputs = len(scalars) + len(arrays)

    def body(*refs):
        tied_refs = refs[inputs : inputs + len(tied)]
        rest = refs[inputs + len(tied) + len(after) :]
        kernel(*refs[:inputs], *rest[: len(outs)], *rest[len(outs) + len(tied) :])
        for source, target in zip(tied_refs, rest[len(outs) :]):
            target[...] = source[...]

    found = pl.pallas_call(
        body,
        out_shape=[*outs, *(jax.ShapeDtypeStruct(t.shape, t.dtype) for t in tied)],
        in_specs=[SMEM] * len(scalars)
        + [VMEM] * (len(arrays) + len(tied))
        + [ANY] * len(after),
        out_specs=[VMEM] * (len(outs) + len(tied)),
        scratch_shapes=list(scratch),
        compiler_params=pltpu.CompilerParams(vmem_limit_bytes=16 * 2**20),
        cost_estimate=pl.CostEstimate(flops=flops, bytes_accessed=moved, transcendentals=0),
    )(*scalars, *arrays, *tied, *after)
    return found[0] if len(found) == 1 else list(found)


def block(*shape):
    return jax.ShapeDtypeStruct(shape, BF)


def either(core_ref, number, work):
    for n in range(2):
        pl.when(core_ref[0] == (number ^ n))(functools.partial(work, n))


def self_energy_patch(spots, scalars, above_by, below_by, pieces, results):
    rows, width = above_by.shape[1:]

    def kernel(*refs):
        refs = list(refs)
        scalar_refs = [refs.pop(0) for _ in scalars]
        above_ref, below_ref = refs.pop(0), refs.pop(0)
        table = refs.pop()
        notes = []
        for n in range(len(pieces)):
            piece_ref = refs.pop(0)
            for each in range(4):
                table[2 * n + each // 2, each % 2] = piece_ref[each * rows : (each + 1) * rows]
            if pieces[n].shape[0] > 4 * rows:
                notes.append(piece_ref[4 * rows : 4 * rows + 16, :128].astype(jnp.int32))
        places = spots(scalar_refs, notes)
        step = 16

        def strip(i, carry):
            at = pl.ds(pl.multiple_of(i * step, step), step)
            factors = [
                (above_ref[m, at, :], below_ref[m, at, :]) for m in range(MODES)
            ]
            for n in range(results):
                for part in range(2):
                    total = None
                    for m in range(MODES):
                        for place, factor in zip(places[n][m], factors[m]):
                            term = factor * table[place, part, at, :].astype(F32)
                            total = term if total is None else total + term
                    refs[n][part, at, :] = total.astype(BF)
            return carry

        lax.fori_loop(0, rows // step, strip, 0)

    return call(
        kernel,
        [block(2, rows, width)] * results,
        scalars,
        [above_by, below_by, *pieces],
        results * 2 * rows * width * 12,
        [pltpu.VMEM((2 * len(pieces), 2, rows, width), BF)],
    )


def rows_at(pieces, part, i, tile):
    n, at = divmod(i, pieces[0].shape[1])
    return pieces[n], (part, slice(at, at + tile), slice(None))


def rows_in(pieces, part, i, tile):
    ref, at = rows_at(pieces, part, i, tile)
    return ref[at]


def put_rows(pieces, part, i, tile, value):
    ref, at = rows_at(pieces, part, i, tile)
    ref[at] = value.astype(BF)


def times_into(left, right, outs):
    size = left.shape[1]
    tile = min(256, outs[0].shape[1])
    real, imag = right[0], right[1]
    for i in range(0, size, tile):
        lr, li = left[0, i : i + tile, :], left[1, i : i + tile, :]
        put_rows(outs, 0, i, tile, dot(lr, real) - dot(li, imag))
        put_rows(outs, 1, i, tile, dot(lr, imag) + dot(li, real))


def times(core, number, lefts, groups, places=None, after=(), tied=()):
    size = lefts[0].shape[1]
    rows, width = groups[0][0].shape[1:]
    full = (2, rows * len(groups), width)
    counts = [len(group) for group in groups]
    scalars = [core] if places is None else [core, places]
    whole = counts == [1]

    def kernel(core_ref, *refs):
        refs = list(refs)
        places_ref = refs.pop(0) if places is not None else None
        left_refs = [refs.pop(0) for _ in range(2)]
        if whole:
            right, *out_refs = refs
        else:
            right = refs.pop()
            out_refs = refs[-CUTS:]
            for n, count in enumerate(counts):
                if places_ref is None:
                    at = slice(n * rows, (n + 1) * rows)
                else:
                    at = pl.ds(pl.multiple_of(places_ref[n] * rows, rows), rows)
                value = refs.pop(0)[...]
                for _ in range(count - 1):
                    value = value + refs.pop(0)[...]
                right[:, at, :] = value
        either(core_ref, number, lambda n: times_into(left_refs[n], right, out_refs))

    return call(
        kernel,
        [block(2, size // CUTS, width)] * CUTS,
        scalars,
        [*lefts, *sum(groups, [])],
        8 * size * size * width,
        [] if whole else [pltpu.VMEM(full, BF)],
        after,
        tied,
    )


def transfer_of(green, coupling, copies=1, after=()):
    size = coupling.shape[0]

    def kernel(green_ref, coupling_ref, *out_refs):
        for part in range(2):
            value = dot(green_ref[part], coupling_ref[...]).astype(BF)
            for out_ref in out_refs:
                out_ref[part] = value

    outs = [block(*green.shape)] * copies
    return call(kernel, outs, [], [green, coupling], 4 * size**3, (), after)


def composed(wanted, left, groups, after=()):
    size = left.shape[1]

    def kernel(wanted_ref, left_ref, *refs):
        *right_refs, out_ref, right = refs

        @pl.when(wanted_ref[0] == 1)
        def _():
            value = right_refs[0][...]
            for ref in right_refs[1:]:
                value = value + ref[...]
            right[...] = value
            times_into(left_ref, right, [out_ref])

        @pl.when(wanted_ref[0] != 1)
        def _():
            out_ref[...] = left_ref[...]

    return call(
        kernel,
        [block(*left.shape)],
        [wanted],
        [left, *groups],
        8 * size**3,
        [pltpu.VMEM(left.shape, BF)],
        after,
    )


def adjoint_into(mine, theirs, right, mine_at, theirs_at, to_at, store):
    size = right.shape[1]
    tile = min(256, mine[0].shape[1])
    a = [right[p, to_at, mine_at] for p in range(2)]
    b = [right[p, to_at, theirs_at] for p in range(2)]
    for i in range(0, size, tile):
        mr, mi = (rows_in(mine, part, i, tile) for part in range(2))
        tr, ti = (rows_in(theirs, part, i, tile) for part in range(2))
        real = dot_t(mr, a[0]) + dot_t(mi, a[1]) + dot_t(tr, b[0]) + dot_t(ti, b[1])
        imag = dot_t(mi, a[0]) - dot_t(mr, a[1]) + dot_t(ti, b[0]) - dot_t(tr, b[1])
        store(i, tile, real, imag)


def split(refs, *counts):
    refs, found = list(refs), []
    for count in counts:
        found.append(refs[:count])
        refs = refs[count:]
    return *found, refs


def adjoint_half(core, number, mine, theirs, rights, summand=(), cuts=1, after=()):
    half, size = mine[0].shape[2], rights[0].shape[1]

    def kernel(core_ref, *refs):
        mine_refs, theirs_refs, right_refs, sum_refs, out_refs = split(
            refs, len(mine), len(theirs), 2, len(summand)
        )

        def store(i, tile, *values):
            for part, value in enumerate(values):
                if sum_refs:
                    value = value + rows_in(sum_refs, part, i, tile).astype(F32)
                put_rows(out_refs, part, i, tile, value)

        def work(n):
            held = number ^ n
            own = slice(held * half, (held + 1) * half)
            other = slice((1 - held) * half, (2 - held) * half)
            adjoint_into(mine_refs, theirs_refs, right_refs[n], own, other, own, store)

        either(core_ref, number, work)

    arrays = [*mine, *theirs, *rights, *summand]
    found = call(
        kernel, [block(2, size // cuts, half)] * cuts, [core], arrays, 16 * size * half * half, (), after
    )
    return [found] if cuts == 1 else list(found)


def adjoint_own(core, mines, theirs, right, sums, other_sums):
    half, size = mines[0][0].shape[2], right.shape[1]
    lists = [*mines, *theirs, *sums, *other_sums]

    def kernel(core_ref, right_ref, *refs):
        *groups, (out_ref,) = split(refs, *(len(each) for each in lists))

        def work(n):
            mine_refs, theirs_refs, sum_refs, other_refs = groups[n::2]
            own, other = slice(n * half, (n + 1) * half), slice((1 - n) * half, (2 - n) * half)
            for to, summand in ((own, sum_refs), (other, other_refs)):

                def store(i, tile, *values):
                    for part, value in enumerate(values):
                        value = value + rows_in(summand, part, i, tile).astype(F32)
                        out_ref[part, i : i + tile, to] = value.astype(BF)

                adjoint_into(mine_refs, theirs_refs, right_ref, own, other, to, store)

        either(core_ref, 0, work)

    out = jax.ShapeDtypeStruct((2, size, size), BF)
    return call(kernel, [out], [core], [right, *sum(lists, [])], 8 * size**3)


def on_device(left_green, coupling, previous_lesser, screened, offsets, occupation):
    energies, slabs = lax.axis_size("energy"), lax.axis_size("slab")
    me, slab = lax.axis_index("energy"), lax.axis_index("slab")
    pairs = energies // 2
    pair, core = me // 2, me % 2
    first = core == 0
    size = coupling.shape[1]
    half = size // 2
    core_s = core[None]

    def swap(value):
        return lax.ppermute(value, "energy", [(i, i ^ 1) for i in range(energies)])

    def to_even(value):
        return lax.ppermute(value, "energy", [(i + 1, i) for i in range(0, energies, 2)])

    def to_odd(value):
        return lax.ppermute(value, "energy", [(i, i + 1) for i in range(0, energies, 2)])

    def by_energy(own, other):
        return jnp.where(first, own, other), jnp.where(first, other, own)

    green = left_green[:, 0, 0]
    before = previous_lesser[:, 0, 0]

    def column_half(value):
        return lax.dynamic_slice_in_dim(value, core * half, half, value.ndim - 1)

    both = [before, swap(before)]
    two = jnp.concatenate([offsets, swap(offsets)])
    spread = pairs in (2, 4) and size % (16 * pairs) == 0
    if spread:
        rows = size // pairs

        def across(value, d):
            moves = [(i, i ^ (2 * d)) for i in range(energies)]
            return lax.ppermute(value, "energy", moves)

        def patch(value, which):
            corner = (0, which * rows, core * half)
            return lax.dynamic_slice(value, corner, (2, rows, half))

        notes = jnp.pad(two.reshape(2 * MODES, 1).astype(BF), ((0, 16 - 2 * MODES), (0, 0)))
        notes = jnp.broadcast_to(notes, (16, half))
        order = list(reversed(range(1, pairs)))

        def patches(which):
            return jnp.concatenate(
                [patch(value, which).reshape(2 * rows, half) for value in both] + [notes]
            )

        sent = [patches(pair ^ d) for d in range(pairs)]
        pieces = sent[:1] + [None] * (pairs - 1)
        for d in order:
            pieces[d] = across(sent[d], d)
        first_sent = sent[1:]
        weights = patch(screened[:, 0], pair)
        places = pair ^ jnp.arange(pairs, dtype=jnp.int32)
        scalars = [me[None]]

        def spots(scalar_refs, carrier_refs):
            here = scalar_refs[0][0]
            found = [[None] * pairs for _ in range(2)]
            core_here = lax.rem(here, 2)
            for d in range(pairs):
                note = carrier_refs[d]
                line = lax.broadcasted_iota(jnp.int32, note.shape, 0)
                for n in range(2):
                    holder = here ^ (2 * d) ^ (core_here ^ n)
                    at = []
                    for m in range(MODES):
                        wanted_line = MODES * (core_here ^ n) + m
                        o = jnp.max(jnp.where(line == wanted_line, note, 0))
                        higher = lax.rem(holder + o, energies) ^ here
                        lower = lax.rem(holder - o + energies, energies) ^ here
                        at.append((higher, lower))
                    found[n][d] = at
            return found[0] + found[1]
    else:
        near = (REACH + 1) // 2
        pieces = []
        for d in range(-near, near + 1):
            moves = [(i, (i - 2 * d) % energies) for i in range(energies)]
            value = jnp.concatenate([column_half(v).reshape(2 * size, half) for v in both])
            pieces.append(lax.ppermute(value, "energy", moves) if d else value)
        weights = column_half(screened[:, 0])
        places, first_sent = None, []
        scalars = [core_s, two]

        def spots(scalar_refs, piece_refs):
            core_ref, two_ref = scalar_refs

            def place(away):
                away = away + 2 * near
                return 2 * lax.div(away, 2) + (lax.rem(away, 2) ^ core_ref[0])

            found = []
            for n in range(2):
                shift = [two_ref[core_ref[0] ^ n, m] for m in range(MODES)]
                found.append([(place(n + o), place(n - o)) for o in shift])
            return found

    own, own_sent = transfer_of(green, coupling[0], 2, first_sent)

    def maps_before(span, own):
        found, moving = [], own
        for hop in range(span):
            moves = [
                (s + hop - 1, s + hop)
                for s in range(3 * span, slabs, 2 * span)
                if s + hop < slabs
            ]
            moving = lax.ppermute(moving, "slab", moves)
            found.append(moving)
        return found

    def swap_all(values):
        return [swap(value) for value in values]

    def arrivals(span, values):
        groups = []
        for moving in values:
            group = []
            for hop in range(span):
                moves = [
                    (s + hop - 1, s + hop)
                    for s in range(span, slabs, 2 * span)
                    if s + hop < slabs
                ]
                moving = lax.ppermute(moving, "slab", moves)
                group.append(moving)
            groups.append(group)
        return groups

    other_green = swap(green)
    lefts = (green, other_green)
    above_by = weights.astype(F32)
    below_by = above_by * occupation[:, None, None]
    found = self_energy_patch(
        spots, scalars, above_by, below_by, pieces, 2 * pairs if spread else 2
    )
    maps = (own, transfer_of(other_green, coupling[0], 1, found[:1]))
    befores = maps_before(1, own_sent) if slabs > 2 else []
    if spread:
        early, late = list(found[:pairs]), list(found[pairs:])
        for d in order:
            early[d] = across(early[d], d)
        early = [[part] for part in early]
        *product, late[1], late[2:] = (
            lambda out: (*out[:CUTS], out[CUTS], list(out[CUTS + 1 :]))
        )(times(core_s, 0, lefts, early, places, maps[1:], late[1:]))
        for d in order:
            late[d] = across(late[d], d)
    else:
        product = times(core_s, 0, lefts, [[found[0]]], None, maps[1:])
        late = [found[1]]
    sums = [adjoint_half(core_s, 0, product, swap_all(product), lefts, (), 1, befores)]
    groups = [arrivals(1, sums[0])]
    product = times(core_s, 1, lefts, [[part] for part in late], places, sums[0])
    sums.append(adjoint_half(core_s, 1, product, swap_all(product), lefts))
    groups.append(arrivals(1, sums[1]))

    span = 1
    while 2 * span < slabs:
        carried = times(core_s, 0, maps, groups[0])
        early = adjoint_half(core_s, 0, carried, swap_all(carried), maps, sums[0], PARTS)
        early_groups = arrivals(2 * span, early)
        wanted = lax.rem(slab // span, 2)[None]
        own = composed(wanted, own, befores, after=early)
        ahead = [group[0] for group in early_groups]
        carried = times(core_s, 1, maps, groups[1], None, [own, *early, *ahead[:AHEAD]])
        behind = ahead[AHEAD:]
        late = adjoint_half(core_s, 1, carried, swap_all(carried), maps, sums[1], 2, behind)
        sums, groups = [early, late], [early_groups, arrivals(2 * span, late)]
        maps = (own, swap(own))
        span *= 2
        if 2 * span < slabs:
            befores = maps_before(span, own)
    if slabs > 1:
        others = [swap_all(value) for value in sums]
        carried = [times(core_s, n, maps, groups[n]) for n in range(2)]
        theirs = [swap_all(value) for value in carried]
        result = adjoint_own(core_s, carried, theirs, maps[0], sums, others)
        return result[:, None, None]
    sums = [value[0] for value in sums]
    result = jnp.where(first, sums[0], sums[1])
    other = swap(jnp.where(first, sums[1], sums[0]))
    return jnp.concatenate(by_energy(result, other), axis=2)[:, None, None]


def solution(mesh):
    placed = (
        P(None, "energy", "slab", None, None),
        P("slab", None, None),
        P(None, "energy", "slab", None, None),
        P(None, "slab", None, None),
        P("energy", None),
        P(),
    )
    return jax.shard_map(
        on_device,
        mesh=mesh,
        in_specs=placed,
        out_specs=P(None, "energy", "slab", None, None),
        check_vma=False,
    )
```

```python
import functools

import jax
import jax.numpy as jnp
from jax import lax
from jax.experimental import pallas as pl
from jax.experimental.pallas import tpu as pltpu
from jax.sharding import PartitionSpec as P

MODES = 2
REACH = 3
BF = jnp.bfloat16
F32 = jnp.float32
CUTS = 2
PARTS = 1
AHEAD = 0

VMEM = pl.BlockSpec(memory_space=pltpu.VMEM)
SMEM = pl.BlockSpec(memory_space=pltpu.SMEM)
ANY = pl.BlockSpec(memory_space=pl.ANY)


def dot(left, right):
    return jnp.dot(left, right, preferred_element_type=F32)


def dot_t(left, right):
    return lax.dot_general(left, right, (((1,), (1,)), ((), ())), preferred_element_type=F32)


def call(kernel, outs, scalars, arrays, flops, scratch=(), after=(), tied=(), to_hbm=False):
    moved = sum(a.size * a.dtype.itemsize for a in [*arrays, *outs])
    inputs = len(scalars) + len(arrays)

    def body(*refs):
        tied_refs = refs[inputs : inputs + len(tied)]
        rest = refs[inputs + len(tied) + len(after) :]
        kernel(*refs[:inputs], *rest[: len(outs)], *rest[len(outs) + len(tied) :])
        for source, target in zip(tied_refs, rest[len(outs) :]):
            target[...] = source[...]

    found = pl.pallas_call(
        body,
        out_shape=[*outs, *(jax.ShapeDtypeStruct(t.shape, t.dtype) for t in tied)],
        in_specs=[SMEM] * len(scalars)
        + [VMEM] * (len(arrays) + len(tied))
        + [ANY] * len(after),
        out_specs=[ANY if to_hbm else VMEM] * (len(outs) + len(tied)),
        scratch_shapes=list(scratch),
        compiler_params=pltpu.CompilerParams(vmem_limit_bytes=16 * 2**20),
        cost_estimate=pl.CostEstimate(flops=flops, bytes_accessed=moved, transcendentals=0),
    )(*scalars, *arrays, *tied, *after)
    return found[0] if len(found) == 1 else list(found)


def block(*shape):
    return jax.ShapeDtypeStruct(shape, BF)


def either(core_ref, number, work):
    for n in range(2):
        pl.when(core_ref[0] == (number ^ n))(functools.partial(work, n))


def self_energy_patch(spots, scalars, above_by, below_by, pieces, results):
    rows, width = above_by.shape[1:]

    def kernel(*refs):
        refs = list(refs)
        scalar_refs = [refs.pop(0) for _ in scalars]
        above_ref, below_ref = refs.pop(0), refs.pop(0)
        table = refs.pop()
        notes = []
        for n in range(len(pieces)):
            piece_ref = refs.pop(0)
            for each in range(4):
                table[2 * n + each // 2, each % 2] = piece_ref[each * rows : (each + 1) * rows]
            if pieces[n].shape[0] > 4 * rows:
                notes.append(piece_ref[4 * rows : 4 * rows + 16, :128].astype(jnp.int32))
        places = spots(scalar_refs, notes)
        step = 16

        def strip(i, carry):
            at = pl.ds(pl.multiple_of(i * step, step), step)
            factors = [
                (above_ref[m, at, :], below_ref[m, at, :]) for m in range(MODES)
            ]
            for n in range(results):
                for part in range(2):
                    total = None
                    for m in range(MODES):
                        for place, factor in zip(places[n][m], factors[m]):
                            term = factor * table[place, part, at, :].astype(F32)
                            total = term if total is None else total + term
                    refs[n][part, at, :] = total.astype(BF)
            return carry

        lax.fori_loop(0, rows // step, strip, 0)

    return call(
        kernel,
        [block(2, rows, width)] * results,
        scalars,
        [above_by, below_by, *pieces],
        results * 2 * rows * width * 12,
        [pltpu.VMEM((2 * len(pieces), 2, rows, width), BF)],
    )


def rows_at(pieces, part, i, tile):
    n, at = divmod(i, pieces[0].shape[1])
    return pieces[n], (part, slice(at, at + tile), slice(None))


def rows_in(pieces, part, i, tile):
    ref, at = rows_at(pieces, part, i, tile)
    return ref[at]


def put_rows(pieces, part, i, tile, value):
    ref, at = rows_at(pieces, part, i, tile)
    ref[at] = value.astype(BF)


def times_into(left, right, outs):
    size = left.shape[1]
    tile = min(256, outs[0].shape[1])
    real, imag = right[0], right[1]
    for i in range(0, size, tile):
        lr, li = left[0, i : i + tile, :], left[1, i : i + tile, :]
        put_rows(outs, 0, i, tile, dot(lr, real) - dot(li, imag))
        put_rows(outs, 1, i, tile, dot(lr, imag) + dot(li, real))


def times(core, number, lefts, groups, places=None, after=(), tied=()):
    size = lefts[0].shape[1]
    rows, width = groups[0][0].shape[1:]
    full = (2, rows * len(groups), width)
    counts = [len(group) for group in groups]
    scalars = [core] if places is None else [core, places]
    whole = counts == [1]

    def kernel(core_ref, *refs):
        refs = list(refs)
        places_ref = refs.pop(0) if places is not None else None
        left_refs = [refs.pop(0) for _ in range(2)]
        if whole:
            right, *out_refs = refs
        else:
            right = refs.pop()
            out_refs = refs[-CUTS:]
            for n, count in enumerate(counts):
                if places_ref is None:
                    at = slice(n * rows, (n + 1) * rows)
                else:
                    at = pl.ds(pl.multiple_of(places_ref[n] * rows, rows), rows)
                value = refs.pop(0)[...]
                for _ in range(count - 1):
                    value = value + refs.pop(0)[...]
                right[:, at, :] = value
        either(core_ref, number, lambda n: times_into(left_refs[n], right, out_refs))

    return call(
        kernel,
        [block(2, size // CUTS, width)] * CUTS,
        scalars,
        [*lefts, *sum(groups, [])],
        8 * size * size * width,
        [] if whole else [pltpu.VMEM(full, BF)],
        after,
        tied,
    )


def transfer_of(green, coupling, copies=1, after=()):
    size = coupling.shape[0]

    def kernel(green_ref, coupling_ref, *out_refs):
        for part in range(2):
            value = dot(green_ref[part], coupling_ref[...]).astype(BF)
            for out_ref in out_refs:
                out_ref[part] = value

    outs = [block(*green.shape)] * copies
    return call(kernel, outs, [], [green, coupling], 4 * size**3, (), after)


def composed(wanted, left, groups, after=()):
    size = left.shape[1]

    def kernel(wanted_ref, left_ref, *refs):
        *right_refs, out_ref, right = refs

        @pl.when(wanted_ref[0] == 1)
        def _():
            value = right_refs[0][...]
            for ref in right_refs[1:]:
                value = value + ref[...]
            right[...] = value
            times_into(left_ref, right, [out_ref])

        @pl.when(wanted_ref[0] != 1)
        def _():
            out_ref[...] = left_ref[...]

    return call(
        kernel,
        [block(*left.shape)],
        [wanted],
        [left, *groups],
        8 * size**3,
        [pltpu.VMEM(left.shape, BF)],
        after,
    )


def adjoint_into(mine, theirs, right, mine_at, theirs_at, to_at, store, span=None):
    size = right.shape[1]
    tile = min(256, mine[0].shape[1])
    a = [right[p, to_at, mine_at] for p in range(2)]
    b = [right[p, to_at, theirs_at] for p in range(2)]
    for i in range(*(span or (0, size)), tile):
        mr, mi = (rows_in(mine, part, i, tile) for part in range(2))
        tr, ti = (rows_in(theirs, part, i, tile) for part in range(2))
        real = dot_t(mr, a[0]) + dot_t(mi, a[1]) + dot_t(tr, b[0]) + dot_t(ti, b[1])
        imag = dot_t(mi, a[0]) - dot_t(mr, a[1]) + dot_t(ti, b[0]) - dot_t(tr, b[1])
        store(i, tile, real, imag)


def split(refs, *counts):
    refs, found = list(refs), []
    for count in counts:
        found.append(refs[:count])
        refs = refs[count:]
    return *found, refs


def adjoint_half(core, number, mine, theirs, rights, summand=(), cuts=1, after=(), copies=1):
    half, size = mine[0].shape[2], rights[0].shape[1]

    def kernel(core_ref, *refs):
        mine_refs, theirs_refs, right_refs, sum_refs, out_refs = split(
            refs, len(mine), len(theirs), 2, len(summand)
        )

        def store(i, tile, *values):
            for part, value in enumerate(values):
                if sum_refs:
                    value = value + rows_in(sum_refs, part, i, tile).astype(F32)
                for n in range(copies):
                    put_rows(out_refs[n * cuts : (n + 1) * cuts], part, i, tile, value)

        def work(n):
            held = number ^ n
            own = slice(held * half, (held + 1) * half)
            other = slice((1 - held) * half, (2 - held) * half)
            adjoint_into(mine_refs, theirs_refs, right_refs[n], own, other, own, store)

        either(core_ref, number, work)

    arrays = [*mine, *theirs, *rights, *summand]
    found = call(
        kernel,
        [block(2, size // cuts, half)] * (cuts * copies),
        [core],
        arrays,
        16 * size * half * half,
        (),
        after,
    )
    if copies == 2:
        return found[:cuts], found[cuts:]
    return [found] if cuts == 1 else list(found)


def adjoint_own(core, mines, theirs, right, sums, other_sums):
    half, size = mines[0][0].shape[2], right.shape[1]
    lists = [*mines, *theirs, *sums, *other_sums]

    def kernel(core_ref, right_ref, *refs):
        *groups, (out_ref, held, sem) = split(refs, *(len(each) for each in lists))
        tile = min(256, mines[0][0].shape[1])

        def moved(i):
            at = slice(i, i + tile)
            return pltpu.make_async_copy(
                held.at[:, at, :], out_ref.at[:, at, :], sem.at[i // tile]
            )

        def work(n):
            mine_refs, theirs_refs, sum_refs, other_refs = groups[n::2]
            own, other = slice(n * half, (n + 1) * half), slice((1 - n) * half, (2 - n) * half)
            for i in range(0, size, tile):
                for to, summand in ((own, sum_refs), (other, other_refs)):

                    def store(i, tile, *values):
                        for part, value in enumerate(values):
                            value = value + rows_in(summand, part, i, tile).astype(F32)
                            held[part, i : i + tile, to] = value.astype(BF)

                    adjoint_into(mine_refs, theirs_refs, right_ref, own, other, to, store, (i, i + tile))
                moved(i).start()

        either(core_ref, 0, work)
        for i in range(0, size, tile):
            moved(i).wait()

    out = jax.ShapeDtypeStruct((2, size, size), BF)
    steps = size // min(256, mines[0][0].shape[1])
    scratch = [pltpu.VMEM(out.shape, BF), pltpu.SemaphoreType.DMA((steps,))]
    return call(
        kernel, [out], [core], [right, *sum(lists, [])], 8 * size**3, scratch, to_hbm=True
    )


def on_device(left_green, coupling, previous_lesser, screened, offsets, occupation):
    energies, slabs = lax.axis_size("energy"), lax.axis_size("slab")
    me, slab = lax.axis_index("energy"), lax.axis_index("slab")
    pairs = energies // 2
    pair, core = me // 2, me % 2
    first = core == 0
    size = coupling.shape[1]
    half = size // 2
    core_s = core[None]

    def swap(value):
        return lax.ppermute(value, "energy", [(i, i ^ 1) for i in range(energies)])

    def to_even(value):
        return lax.ppermute(value, "energy", [(i + 1, i) for i in range(0, energies, 2)])

    def to_odd(value):
        return lax.ppermute(value, "energy", [(i, i + 1) for i in range(0, energies, 2)])

    def by_energy(own, other):
        return jnp.where(first, own, other), jnp.where(first, other, own)

    green = left_green[:, 0, 0]
    before = previous_lesser[:, 0, 0]

    def column_half(value):
        return lax.dynamic_slice_in_dim(value, core * half, half, value.ndim - 1)

    both = [before, swap(before)]
    two = jnp.concatenate([offsets, swap(offsets)])
    spread = pairs in (2, 4) and size % (16 * pairs) == 0
    if spread:
        rows = size // pairs

        def across(value, d):
            moves = [(i, i ^ (2 * d)) for i in range(energies)]
            return lax.ppermute(value, "energy", moves)

        def patch(value, which):
            corner = (0, which * rows, core * half)
            return lax.dynamic_slice(value, corner, (2, rows, half))

        notes = jnp.pad(two.reshape(2 * MODES, 1).astype(BF), ((0, 16 - 2 * MODES), (0, 0)))
        notes = jnp.broadcast_to(notes, (16, half))
        order = list(reversed(range(1, pairs)))

        def patches(which):
            return jnp.concatenate(
                [patch(value, which).reshape(2 * rows, half) for value in both] + [notes]
            )

        sent = [patches(pair ^ d) for d in range(pairs)]
        pieces = sent[:1] + [None] * (pairs - 1)
        for d in order:
            pieces[d] = across(sent[d], d)
        first_sent = sent[1:]
        weights = patch(screened[:, 0], pair)
        places = pair ^ jnp.arange(pairs, dtype=jnp.int32)
        scalars = [me[None]]

        def spots(scalar_refs, carrier_refs):
            here = scalar_refs[0][0]
            found = [[None] * pairs for _ in range(2)]
            core_here = lax.rem(here, 2)
            for d in range(pairs):
                note = carrier_refs[d]
                line = lax.broadcasted_iota(jnp.int32, note.shape, 0)
                for n in range(2):
                    holder = here ^ (2 * d) ^ (core_here ^ n)
                    at = []
                    for m in range(MODES):
                        wanted_line = MODES * (core_here ^ n) + m
                        o = jnp.max(jnp.where(line == wanted_line, note, 0))
                        higher = lax.rem(holder + o, energies) ^ here
                        lower = lax.rem(holder - o + energies, energies) ^ here
                        at.append((higher, lower))
                    found[n][d] = at
            return found[0] + found[1]
    else:
        near = (REACH + 1) // 2
        pieces = []
        for d in range(-near, near + 1):
            moves = [(i, (i - 2 * d) % energies) for i in range(energies)]
            value = jnp.concatenate([column_half(v).reshape(2 * size, half) for v in both])
            pieces.append(lax.ppermute(value, "energy", moves) if d else value)
        weights = column_half(screened[:, 0])
        places, first_sent = None, []
        scalars = [core_s, two]

        def spots(scalar_refs, piece_refs):
            core_ref, two_ref = scalar_refs

            def place(away):
                away = away + 2 * near
                return 2 * lax.div(away, 2) + (lax.rem(away, 2) ^ core_ref[0])

            found = []
            for n in range(2):
                shift = [two_ref[core_ref[0] ^ n, m] for m in range(MODES)]
                found.append([(place(n + o), place(n - o)) for o in shift])
            return found

    own, own_sent = transfer_of(green, coupling[0], 2, first_sent)

    def maps_before(span, own):
        found, moving = [], own
        for hop in range(span):
            moves = [
                (s + hop - 1, s + hop)
                for s in range(3 * span, slabs, 2 * span)
                if s + hop < slabs
            ]
            moving = lax.ppermute(moving, "slab", moves)
            found.append(moving)
        return found

    def swap_all(values):
        return [swap(value) for value in values]

    def arrivals(span, values):
        groups = []
        for moving in values:
            group = []
            for hop in range(span):
                moves = [
                    (s + hop - 1, s + hop)
                    for s in range(span, slabs, 2 * span)
                    if s + hop < slabs
                ]
                moving = lax.ppermute(moving, "slab", moves)
                group.append(moving)
            groups.append(group)
        return groups

    other_green = swap(green)
    lefts = (green, other_green)
    above_by = weights.astype(F32)
    below_by = above_by * occupation[:, None, None]
    found = self_energy_patch(
        spots, scalars, above_by, below_by, pieces, 2 * pairs if spread else 2
    )
    maps = (own, transfer_of(other_green, coupling[0], 1, found[:1]))
    befores = maps_before(1, own_sent) if slabs > 2 else []
    if spread:
        early, late = list(found[:pairs]), list(found[pairs:])
        for d in order:
            early[d] = across(early[d], d)
        early = [[part] for part in early]
        *product, late[1], late[2:] = (
            lambda out: (*out[:CUTS], out[CUTS], list(out[CUTS + 1 :]))
        )(times(core_s, 0, lefts, early, places, maps[1:], late[1:]))
        for d in order:
            late[d] = across(late[d], d)
    else:
        product = times(core_s, 0, lefts, [[found[0]]], None, maps[1:])
        late = [found[1]]
    sums = [adjoint_half(core_s, 0, product, swap_all(product), lefts, (), 1, befores)]
    groups = [arrivals(1, sums[0])]
    product = times(core_s, 1, lefts, [[part] for part in late], places, sums[0])
    source, source_sent = adjoint_half(
        core_s, 1, product, swap_all(product), lefts, copies=2
    )
    sums.append(source)
    groups.append(arrivals(1, source_sent))

    span = 1
    while 2 * span < slabs:
        carried = times(core_s, 0, maps, groups[0], None, sums[1])
        early, early_sent = adjoint_half(
            core_s, 0, carried, swap_all(carried), maps, sums[0], PARTS, copies=2
        )
        early_groups = arrivals(2 * span, early_sent)
        wanted = lax.rem(slab // span, 2)[None]
        own = composed(wanted, own, befores, after=early)
        ahead = [group[0] for group in early_groups]
        carried = times(core_s, 1, maps, groups[1], None, [own, *early, *ahead[:AHEAD]])
        behind = ahead[AHEAD:]
        late = adjoint_half(core_s, 1, carried, swap_all(carried), maps, sums[1], 2, behind)
        sums, groups = [early, late], [early_groups, arrivals(2 * span, late)]
        maps = (own, swap(own))
        span *= 2
        if 2 * span < slabs:
            befores = maps_before(span, own)
    if slabs > 1:
        others = [swap_all(value) for value in sums]
        carried = [times(core_s, n, maps, groups[n]) for n in range(2)]
        theirs = [swap_all(value) for value in carried]
        result = adjoint_own(core_s, carried, theirs, maps[0], sums, others)
        return result[:, None, None]
    sums = [value[0] for value in sums]
    result = jnp.where(first, sums[0], sums[1])
    other = swap(jnp.where(first, sums[1], sums[0]))
    return jnp.concatenate(by_energy(result, other), axis=2)[:, None, None]


def solution(mesh):
    placed = (
        P(None, "energy", "slab", None, None),
        P("slab", None, None),
        P(None, "energy", "slab", None, None),
        P(None, "slab", None, None),
        P("energy", None),
        P(),
    )
    return jax.shard_map(
        on_device,
        mesh=mesh,
        in_specs=placed,
        out_specs=P(None, "energy", "slab", None, None),
        check_vma=False,
    )
```

```python
import functools

import jax
import jax.numpy as jnp
from jax import lax
from jax.experimental import pallas as pl
from jax.experimental.pallas import tpu as pltpu
from jax.sharding import PartitionSpec as P

MODES = 2
REACH = 3
BF = jnp.bfloat16
F32 = jnp.float32
CUTS = 2
PARTS = 1
AHEAD = 0

VMEM = pl.BlockSpec(memory_space=pltpu.VMEM)
SMEM = pl.BlockSpec(memory_space=pltpu.SMEM)
ANY = pl.BlockSpec(memory_space=pl.ANY)


def dot(left, right):
    return jnp.dot(left, right, preferred_element_type=F32)


def dot_t(left, right):
    return lax.dot_general(left, right, (((1,), (1,)), ((), ())), preferred_element_type=F32)


def call(kernel, outs, scalars, arrays, flops, scratch=(), after=(), tied=(), to_hbm=False):
    moved = sum(a.size * a.dtype.itemsize for a in [*arrays, *outs])
    inputs = len(scalars) + len(arrays)

    def body(*refs):
        tied_refs = refs[inputs : inputs + len(tied)]
        rest = refs[inputs + len(tied) + len(after) :]
        kernel(*refs[:inputs], *rest[: len(outs)], *rest[len(outs) + len(tied) :])
        for source, target in zip(tied_refs, rest[len(outs) :]):
            target[...] = source[...]

    found = pl.pallas_call(
        body,
        out_shape=[*outs, *(jax.ShapeDtypeStruct(t.shape, t.dtype) for t in tied)],
        in_specs=[SMEM] * len(scalars)
        + [VMEM] * (len(arrays) + len(tied))
        + [ANY] * len(after),
        out_specs=[ANY if to_hbm else VMEM] * (len(outs) + len(tied)),
        scratch_shapes=list(scratch),
        compiler_params=pltpu.CompilerParams(vmem_limit_bytes=16 * 2**20),
        cost_estimate=pl.CostEstimate(flops=flops, bytes_accessed=moved, transcendentals=0),
    )(*scalars, *arrays, *tied, *after)
    return found[0] if len(found) == 1 else list(found)


def block(*shape):
    return jax.ShapeDtypeStruct(shape, BF)


def either(core_ref, number, work):
    for n in range(2):
        pl.when(core_ref[0] == (number ^ n))(functools.partial(work, n))


def self_energy_patch(spots, scalars, above_by, below_by, pieces, results):
    rows, width = above_by.shape[1:]

    def kernel(*refs):
        refs = list(refs)
        scalar_refs = [refs.pop(0) for _ in scalars]
        above_ref, below_ref = refs.pop(0), refs.pop(0)
        table = refs.pop()
        notes = []
        for n in range(len(pieces)):
            piece_ref = refs.pop(0)
            for each in range(4):
                table[2 * n + each // 2, each % 2] = piece_ref[each * rows : (each + 1) * rows]
            if pieces[n].shape[0] > 4 * rows:
                notes.append(piece_ref[4 * rows : 4 * rows + 16, :128].astype(jnp.int32))
        places = spots(scalar_refs, notes)
        step = 16

        def strip(i, carry):
            at = pl.ds(pl.multiple_of(i * step, step), step)
            factors = [
                (above_ref[m, at, :], below_ref[m, at, :]) for m in range(MODES)
            ]
            for n in range(results):
                for part in range(2):
                    total = None
                    for m in range(MODES):
                        for place, factor in zip(places[n][m], factors[m]):
                            term = factor * table[place, part, at, :].astype(F32)
                            total = term if total is None else total + term
                    refs[n][part, at, :] = total.astype(BF)
            return carry

        lax.fori_loop(0, rows // step, strip, 0)

    return call(
        kernel,
        [block(2, rows, width)] * results,
        scalars,
        [above_by, below_by, *pieces],
        results * 2 * rows * width * 12,
        [pltpu.VMEM((2 * len(pieces), 2, rows, width), BF)],
    )


def rows_at(pieces, part, i, tile):
    n, at = divmod(i, pieces[0].shape[1])
    return pieces[n], (part, slice(at, at + tile), slice(None))


def rows_in(pieces, part, i, tile):
    ref, at = rows_at(pieces, part, i, tile)
    return ref[at]


def put_rows(pieces, part, i, tile, value):
    ref, at = rows_at(pieces, part, i, tile)
    ref[at] = value.astype(BF)


def times_into(left, right, outs):
    size = left.shape[1]
    tile = min(256, outs[0].shape[1])
    real, imag = right[0], right[1]
    for i in range(0, size, tile):
        lr, li = left[0, i : i + tile, :], left[1, i : i + tile, :]
        put_rows(outs, 0, i, tile, dot(lr, real) - dot(li, imag))
        put_rows(outs, 1, i, tile, dot(lr, imag) + dot(li, real))


def times(core, number, lefts, groups, places=None, after=(), tied=()):
    size = lefts[0].shape[1]
    rows, width = groups[0][0].shape[1:]
    full = (2, rows * len(groups), width)
    counts = [len(group) for group in groups]
    scalars = [core] if places is None else [core, places]
    whole = counts == [1]

    def kernel(core_ref, *refs):
        refs = list(refs)
        places_ref = refs.pop(0) if places is not None else None
        left_refs = [refs.pop(0) for _ in range(2)]
        if whole:
            right, *out_refs = refs
        else:
            right = refs.pop()
            out_refs = refs[-CUTS:]
            for n, count in enumerate(counts):
                if places_ref is None:
                    at = slice(n * rows, (n + 1) * rows)
                else:
                    at = pl.ds(pl.multiple_of(places_ref[n] * rows, rows), rows)
                value = refs.pop(0)[...]
                for _ in range(count - 1):
                    value = value + refs.pop(0)[...]
                right[:, at, :] = value
        either(core_ref, number, lambda n: times_into(left_refs[n], right, out_refs))

    return call(
        kernel,
        [block(2, size // CUTS, width)] * CUTS,
        scalars,
        [*lefts, *sum(groups, [])],
        8 * size * size * width,
        [] if whole else [pltpu.VMEM(full, BF)],
        after,
        tied,
    )


def transfer_of(green, coupling, copies=1, after=()):
    size = coupling.shape[0]

    def kernel(green_ref, coupling_ref, *out_refs):
        for part in range(2):
            value = dot(green_ref[part], coupling_ref[...]).astype(BF)
            for out_ref in out_refs:
                out_ref[part] = value

    outs = [block(*green.shape)] * copies
    return call(kernel, outs, [], [green, coupling], 4 * size**3, (), after)


def composed(wanted, left, groups, after=()):
    size = left.shape[1]

    def kernel(wanted_ref, left_ref, *refs):
        *right_refs, out_ref, right = refs

        @pl.when(wanted_ref[0] == 1)
        def _():
            value = right_refs[0][...]
            for ref in right_refs[1:]:
                value = value + ref[...]
            right[...] = value
            times_into(left_ref, right, [out_ref])

        @pl.when(wanted_ref[0] != 1)
        def _():
            out_ref[...] = left_ref[...]

    return call(
        kernel,
        [block(*left.shape)],
        [wanted],
        [left, *groups],
        8 * size**3,
        [pltpu.VMEM(left.shape, BF)],
        after,
    )


def adjoint_into(mine, theirs, right, mine_at, theirs_at, to_at, store, span=None):
    size = right.shape[1]
    tile = min(256, mine[0].shape[1])
    a = [right[p, to_at, mine_at] for p in range(2)]
    b = [right[p, to_at, theirs_at] for p in range(2)]
    for i in range(*(span or (0, size)), tile):
        mr, mi = (rows_in(mine, part, i, tile) for part in range(2))
        tr, ti = (rows_in(theirs, part, i, tile) for part in range(2))
        real = dot_t(mr, a[0]) + dot_t(mi, a[1]) + dot_t(tr, b[0]) + dot_t(ti, b[1])
        imag = dot_t(mi, a[0]) - dot_t(mr, a[1]) + dot_t(ti, b[0]) - dot_t(tr, b[1])
        store(i, tile, real, imag)


def split(refs, *counts):
    refs, found = list(refs), []
    for count in counts:
        found.append(refs[:count])
        refs = refs[count:]
    return *found, refs


def adjoint_half(core, number, mine, theirs, rights, summand=(), cuts=1, after=(), copies=1):
    half, size = mine[0].shape[2], rights[0].shape[1]

    def kernel(core_ref, *refs):
        mine_refs, theirs_refs, right_refs, sum_refs, out_refs = split(
            refs, len(mine), len(theirs), 2, len(summand)
        )

        def store(i, tile, *values):
            for part, value in enumerate(values):
                if sum_refs:
                    value = value + rows_in(sum_refs, part, i, tile).astype(F32)
                for n in range(copies):
                    put_rows(out_refs[n * cuts : (n + 1) * cuts], part, i, tile, value)

        def work(n):
            held = number ^ n
            own = slice(held * half, (held + 1) * half)
            other = slice((1 - held) * half, (2 - held) * half)
            adjoint_into(mine_refs, theirs_refs, right_refs[n], own, other, own, store)

        either(core_ref, number, work)

    arrays = [*mine, *theirs, *rights, *summand]
    found = call(
        kernel,
        [block(2, size // cuts, half)] * (cuts * copies),
        [core],
        arrays,
        16 * size * half * half,
        (),
        after,
    )
    if copies == 2:
        return found[:cuts], found[cuts:]
    return [found] if cuts == 1 else list(found)


def adjoint_own(core, mines, theirs, right, sums, other_sums):
    half, size = mines[0][0].shape[2], right.shape[1]
    lists = [*mines, *theirs, *sums, *other_sums]

    def kernel(core_ref, right_ref, *refs):
        *groups, (out_ref, held, sem) = split(refs, *(len(each) for each in lists))
        tile = min(256, mines[0][0].shape[1])

        def moved(i):
            at = slice(i, i + tile)
            return pltpu.make_async_copy(
                held.at[:, at, :], out_ref.at[:, at, :], sem.at[i // tile]
            )

        def work(n):
            mine_refs, theirs_refs, sum_refs, other_refs = groups[n::2]
            own, other = slice(n * half, (n + 1) * half), slice((1 - n) * half, (2 - n) * half)
            for i in range(0, size, tile):
                for to, summand in ((own, sum_refs), (other, other_refs)):

                    def store(i, tile, *values):
                        for part, value in enumerate(values):
                            value = value + rows_in(summand, part, i, tile).astype(F32)
                            held[part, i : i + tile, to] = value.astype(BF)

                    adjoint_into(mine_refs, theirs_refs, right_ref, own, other, to, store, (i, i + tile))
                moved(i).start()

        either(core_ref, 0, work)
        for i in range(0, size, tile):
            moved(i).wait()

    out = jax.ShapeDtypeStruct((2, size, size), BF)
    steps = size // min(256, mines[0][0].shape[1])
    scratch = [pltpu.VMEM(out.shape, BF), pltpu.SemaphoreType.DMA((steps,))]
    return call(
        kernel, [out], [core], [right, *sum(lists, [])], 8 * size**3, scratch, to_hbm=True
    )


def on_device(left_green, coupling, previous_lesser, screened, offsets, occupation):
    energies, slabs = lax.axis_size("energy"), lax.axis_size("slab")
    me, slab = lax.axis_index("energy"), lax.axis_index("slab")
    pairs = energies // 2
    pair, core = me // 2, me % 2
    first = core == 0
    size = coupling.shape[1]
    half = size // 2
    core_s = core[None]

    def swap(value):
        return lax.ppermute(value, "energy", [(i, i ^ 1) for i in range(energies)])

    def to_even(value):
        return lax.ppermute(value, "energy", [(i + 1, i) for i in range(0, energies, 2)])

    def to_odd(value):
        return lax.ppermute(value, "energy", [(i, i + 1) for i in range(0, energies, 2)])

    def by_energy(own, other):
        return jnp.where(first, own, other), jnp.where(first, other, own)

    green = left_green[:, 0, 0]
    before = previous_lesser[:, 0, 0]

    def column_half(value):
        return lax.dynamic_slice_in_dim(value, core * half, half, value.ndim - 1)

    both = [before, swap(before)]
    two = jnp.concatenate([offsets, swap(offsets)])
    spread = pairs in (2, 4) and size % (16 * pairs) == 0
    if spread:
        rows = size // pairs

        def across(value, d):
            moves = [(i, i ^ (2 * d)) for i in range(energies)]
            return lax.ppermute(value, "energy", moves)

        def patch(value, which):
            corner = (0, which * rows, core * half)
            return lax.dynamic_slice(value, corner, (2, rows, half))

        notes = jnp.pad(two.reshape(2 * MODES, 1).astype(BF), ((0, 16 - 2 * MODES), (0, 0)))
        notes = jnp.broadcast_to(notes, (16, half))
        order = list(reversed(range(1, pairs)))

        def patches(which):
            return jnp.concatenate(
                [patch(value, which).reshape(2 * rows, half) for value in both] + [notes]
            )

        sent = [patches(pair ^ d) for d in range(pairs)]
        pieces = sent[:1] + [None] * (pairs - 1)
        for d in order:
            pieces[d] = across(sent[d], d)
        first_sent = sent[1:]
        weights = patch(screened[:, 0], pair)
        places = pair ^ jnp.arange(pairs, dtype=jnp.int32)
        scalars = [me[None]]

        def spots(scalar_refs, carrier_refs):
            here = scalar_refs[0][0]
            found = [[None] * pairs for _ in range(2)]
            core_here = lax.rem(here, 2)
            for d in range(pairs):
                note = carrier_refs[d]
                line = lax.broadcasted_iota(jnp.int32, note.shape, 0)
                for n in range(2):
                    holder = here ^ (2 * d) ^ (core_here ^ n)
                    at = []
                    for m in range(MODES):
                        wanted_line = MODES * (core_here ^ n) + m
                        o = jnp.max(jnp.where(line == wanted_line, note, 0))
                        higher = lax.rem(holder + o, energies) ^ here
                        lower = lax.rem(holder - o + energies, energies) ^ here
                        at.append((higher, lower))
                    found[n][d] = at
            return found[0] + found[1]
    else:
        near = (REACH + 1) // 2
        pieces = []
        for d in range(-near, near + 1):
            moves = [(i, (i - 2 * d) % energies) for i in range(energies)]
            value = jnp.concatenate([column_half(v).reshape(2 * size, half) for v in both])
            pieces.append(lax.ppermute(value, "energy", moves) if d else value)
        weights = column_half(screened[:, 0])
        places, first_sent = None, []
        scalars = [core_s, two]

        def spots(scalar_refs, piece_refs):
            core_ref, two_ref = scalar_refs

            def place(away):
                away = away + 2 * near
                return 2 * lax.div(away, 2) + (lax.rem(away, 2) ^ core_ref[0])

            found = []
            for n in range(2):
                shift = [two_ref[core_ref[0] ^ n, m] for m in range(MODES)]
                found.append([(place(n + o), place(n - o)) for o in shift])
            return found

    own, own_sent = transfer_of(green, coupling[0], 2, first_sent)

    def maps_before(span, own):
        found, moving = [], own
        for hop in range(span):
            moves = [
                (s + hop - 1, s + hop)
                for s in range(3 * span, slabs, 2 * span)
                if s + hop < slabs
            ]
            moving = lax.ppermute(moving, "slab", moves)
            found.append(moving)
        return found

    def swap_all(values):
        return [swap(value) for value in values]

    def arrivals(span, values):
        groups = []
        for moving in values:
            group = []
            for hop in range(span):
                moves = [
                    (s + hop - 1, s + hop)
                    for s in range(span, slabs, 2 * span)
                    if s + hop < slabs
                ]
                moving = lax.ppermute(moving, "slab", moves)
                group.append(moving)
            groups.append(group)
        return groups

    other_green = swap(green)
    lefts = (green, other_green)
    above_by = weights.astype(F32)
    below_by = above_by * occupation[:, None, None]
    found = self_energy_patch(
        spots, scalars, above_by, below_by, pieces, 2 * pairs if spread else 2
    )
    maps = (own, transfer_of(other_green, coupling[0], 1, found[:1]))
    befores = maps_before(1, own_sent) if slabs > 2 else []
    if spread:
        early, late = list(found[:pairs]), list(found[pairs:])
        for d in order:
            early[d] = across(early[d], d)
        early = [[part] for part in early]
        *product, late[1], late[2:] = (
            lambda out: (*out[:CUTS], out[CUTS], list(out[CUTS + 1 :]))
        )(times(core_s, 0, lefts, early, places, maps[1:], late[1:]))
        for d in order:
            late[d] = across(late[d], d)
    else:
        product = times(core_s, 0, lefts, [[found[0]]], None, maps[1:])
        late = [found[1]]
    sums = [adjoint_half(core_s, 0, product, swap_all(product), lefts)]
    groups = [arrivals(1, sums[0])]
    product = times(core_s, 1, lefts, [[part] for part in late], places, sums[0])
    source, source_sent = adjoint_half(
        core_s, 1, product, swap_all(product), lefts, after=befores, copies=2
    )
    sums.append(source)
    groups.append(arrivals(1, source_sent))

    span = 1
    while 2 * span < slabs:
        carried = times(core_s, 0, maps, groups[0], None, sums[1])
        early, early_sent = adjoint_half(
            core_s, 0, carried, swap_all(carried), maps, sums[0], PARTS, copies=2
        )
        early_groups = arrivals(2 * span, early_sent)
        wanted = lax.rem(slab // span, 2)[None]
        own = composed(wanted, own, befores, after=early)
        ahead = [group[0] for group in early_groups]
        carried = times(core_s, 1, maps, groups[1], None, [own, *early, *ahead[:AHEAD]])
        behind = ahead[AHEAD:]
        late = adjoint_half(core_s, 1, carried, swap_all(carried), maps, sums[1], 2, behind)
        sums, groups = [early, late], [early_groups, arrivals(2 * span, late)]
        maps = (own, swap(own))
        span *= 2
        if 2 * span < slabs:
            befores = maps_before(span, own)
    if slabs > 1:
        others = [swap_all(value) for value in sums]
        carried = [times(core_s, 0, maps, groups[0])]
        theirs = [swap_all(carried[0])]
        carried.append(times(core_s, 1, maps, groups[1], None, theirs[0]))
        theirs.append(swap_all(carried[1]))
        result = adjoint_own(core_s, carried, theirs, maps[0], sums, others)
        return result[:, None, None]
    sums = [value[0] for value in sums]
    result = jnp.where(first, sums[0], sums[1])
    other = swap(jnp.where(first, sums[1], sums[0]))
    return jnp.concatenate(by_energy(result, other), axis=2)[:, None, None]


def solution(mesh):
    placed = (
        P(None, "energy", "slab", None, None),
        P("slab", None, None),
        P(None, "energy", "slab", None, None),
        P(None, "slab", None, None),
        P("energy", None),
        P(),
    )
    return jax.shard_map(
        on_device,
        mesh=mesh,
        in_specs=placed,
        out_specs=P(None, "energy", "slab", None, None),
        check_vma=False,
    )
```

```python
import functools

import jax
import jax.numpy as jnp
from jax import lax
from jax.experimental import pallas as pl
from jax.experimental.pallas import tpu as pltpu
from jax.sharding import PartitionSpec as P

MODES = 2
REACH = 3
BF = jnp.bfloat16
F32 = jnp.float32
CUTS = 2
PARTS = 1
AHEAD = 0

VMEM = pl.BlockSpec(memory_space=pltpu.VMEM)
SMEM = pl.BlockSpec(memory_space=pltpu.SMEM)
ANY = pl.BlockSpec(memory_space=pl.ANY)


def dot(left, right):
    return jnp.dot(left, right, preferred_element_type=F32)


def dot_t(left, right):
    return lax.dot_general(left, right, (((1,), (1,)), ((), ())), preferred_element_type=F32)


def call(kernel, outs, scalars, arrays, flops, scratch=(), after=(), tied=(), to_hbm=False):
    moved = sum(a.size * a.dtype.itemsize for a in [*arrays, *outs])
    inputs = len(scalars) + len(arrays)

    def body(*refs):
        tied_refs = refs[inputs : inputs + len(tied)]
        rest = refs[inputs + len(tied) + len(after) :]
        kernel(*refs[:inputs], *rest[: len(outs)], *rest[len(outs) + len(tied) :])
        for source, target in zip(tied_refs, rest[len(outs) :]):
            target[...] = source[...]

    found = pl.pallas_call(
        body,
        out_shape=[*outs, *(jax.ShapeDtypeStruct(t.shape, t.dtype) for t in tied)],
        in_specs=[SMEM] * len(scalars)
        + [VMEM] * (len(arrays) + len(tied))
        + [ANY] * len(after),
        out_specs=[ANY if to_hbm else VMEM] * (len(outs) + len(tied)),
        scratch_shapes=list(scratch),
        compiler_params=pltpu.CompilerParams(vmem_limit_bytes=16 * 2**20),
        cost_estimate=pl.CostEstimate(flops=flops, bytes_accessed=moved, transcendentals=0),
    )(*scalars, *arrays, *tied, *after)
    return found[0] if len(found) == 1 else list(found)


def block(*shape):
    return jax.ShapeDtypeStruct(shape, BF)


def where_active(active_ref, work, otherwise=None):
    if active_ref is None:
        work()
        return
    pl.when(active_ref[0] == 1)(work)
    if otherwise is not None:
        pl.when(active_ref[0] != 1)(otherwise)


def either(core_ref, number, work):
    for n in range(2):
        pl.when(core_ref[0] == (number ^ n))(functools.partial(work, n))


def self_energy_patch(spots, scalars, above_by, below_by, pieces, results):
    rows, width = above_by.shape[1:]

    def kernel(*refs):
        refs = list(refs)
        scalar_refs = [refs.pop(0) for _ in scalars]
        above_ref, below_ref = refs.pop(0), refs.pop(0)
        table = refs.pop()
        notes = []
        for n in range(len(pieces)):
            piece_ref = refs.pop(0)
            for each in range(4):
                table[2 * n + each // 2, each % 2] = piece_ref[each * rows : (each + 1) * rows]
            if pieces[n].shape[0] > 4 * rows:
                notes.append(piece_ref[4 * rows : 4 * rows + 16, :128].astype(jnp.int32))
        places = spots(scalar_refs, notes)
        step = 16

        def strip(i, carry):
            at = pl.ds(pl.multiple_of(i * step, step), step)
            factors = [
                (above_ref[m, at, :], below_ref[m, at, :]) for m in range(MODES)
            ]
            for n in range(results):
                for part in range(2):
                    total = None
                    for m in range(MODES):
                        for place, factor in zip(places[n][m], factors[m]):
                            term = factor * table[place, part, at, :].astype(F32)
                            total = term if total is None else total + term
                    refs[n][part, at, :] = total.astype(BF)
            return carry

        lax.fori_loop(0, rows // step, strip, 0)

    return call(
        kernel,
        [block(2, rows, width)] * results,
        scalars,
        [above_by, below_by, *pieces],
        results * 2 * rows * width * 12,
        [pltpu.VMEM((2 * len(pieces), 2, rows, width), BF)],
    )


def rows_at(pieces, part, i, tile):
    n, at = divmod(i, pieces[0].shape[1])
    return pieces[n], (part, slice(at, at + tile), slice(None))


def rows_in(pieces, part, i, tile):
    ref, at = rows_at(pieces, part, i, tile)
    return ref[at]


def put_rows(pieces, part, i, tile, value):
    ref, at = rows_at(pieces, part, i, tile)
    ref[at] = value.astype(BF)


def times_into(left, right, outs):
    size = left.shape[1]
    tile = min(256, outs[0].shape[1])
    real, imag = right[0], right[1]
    for i in range(0, size, tile):
        lr, li = left[0, i : i + tile, :], left[1, i : i + tile, :]
        put_rows(outs, 0, i, tile, dot(lr, real) - dot(li, imag))
        put_rows(outs, 1, i, tile, dot(lr, imag) + dot(li, real))


def times(core, number, lefts, groups, places=None, after=(), tied=(), active=None):
    size = lefts[0].shape[1]
    rows, width = groups[0][0].shape[1:]
    full = (2, rows * len(groups), width)
    counts = [len(group) for group in groups]
    scalars = [core] if places is None else [core, places]
    scalars += [] if active is None else [active]
    whole = counts == [1]

    def kernel(core_ref, *refs):
        refs = list(refs)
        places_ref = refs.pop(0) if places is not None else None
        active_ref = refs.pop(0) if active is not None else None
        left_refs = [refs.pop(0) for _ in range(2)]
        if whole:
            right, *out_refs = refs
        else:
            right = refs.pop()
            out_refs = refs[-CUTS:]
            for n, count in enumerate(counts):
                if places_ref is None:
                    at = slice(n * rows, (n + 1) * rows)
                else:
                    at = pl.ds(pl.multiple_of(places_ref[n] * rows, rows), rows)
                value = refs.pop(0)[...]
                for _ in range(count - 1):
                    value = value + refs.pop(0)[...]
                right[:, at, :] = value

        def work():
            either(core_ref, number, lambda n: times_into(left_refs[n], right, out_refs))

        where_active(active_ref, work)

    return call(
        kernel,
        [block(2, size // CUTS, width)] * CUTS,
        scalars,
        [*lefts, *sum(groups, [])],
        8 * size * size * width,
        [] if whole else [pltpu.VMEM(full, BF)],
        after,
        tied,
    )


def transfer_of(green, coupling, copies=1, after=()):
    size = coupling.shape[0]

    def kernel(green_ref, coupling_ref, *out_refs):
        for part in range(2):
            value = dot(green_ref[part], coupling_ref[...]).astype(BF)
            for out_ref in out_refs:
                out_ref[part] = value

    outs = [block(*green.shape)] * copies
    return call(kernel, outs, [], [green, coupling], 4 * size**3, (), after)


def composed(wanted, left, groups, after=()):
    size = left.shape[1]

    def kernel(wanted_ref, left_ref, *refs):
        *right_refs, out_ref, right = refs

        @pl.when(wanted_ref[0] == 1)
        def _():
            value = right_refs[0][...]
            for ref in right_refs[1:]:
                value = value + ref[...]
            right[...] = value
            times_into(left_ref, right, [out_ref])

        @pl.when(wanted_ref[0] != 1)
        def _():
            out_ref[...] = left_ref[...]

    return call(
        kernel,
        [block(*left.shape)],
        [wanted],
        [left, *groups],
        8 * size**3,
        [pltpu.VMEM(left.shape, BF)],
        after,
    )


def adjoint_into(mine, theirs, right, mine_at, theirs_at, to_at, store, span=None):
    size = right.shape[1]
    tile = min(256, mine[0].shape[1])
    a = [right[p, to_at, mine_at] for p in range(2)]
    b = [right[p, to_at, theirs_at] for p in range(2)]
    for i in range(*(span or (0, size)), tile):
        mr, mi = (rows_in(mine, part, i, tile) for part in range(2))
        tr, ti = (rows_in(theirs, part, i, tile) for part in range(2))
        real = dot_t(mr, a[0]) + dot_t(mi, a[1]) + dot_t(tr, b[0]) + dot_t(ti, b[1])
        imag = dot_t(mi, a[0]) - dot_t(mr, a[1]) + dot_t(ti, b[0]) - dot_t(tr, b[1])
        store(i, tile, real, imag)


def split(refs, *counts):
    refs, found = list(refs), []
    for count in counts:
        found.append(refs[:count])
        refs = refs[count:]
    return *found, refs


def adjoint_half(core, number, mine, theirs, rights, summand=(), cuts=1, after=(), copies=1, active=None):
    half, size = mine[0].shape[2], rights[0].shape[1]

    scalars = [core] if active is None else [core, active]

    def kernel(core_ref, *refs):
        active_refs, mine_refs, theirs_refs, right_refs, sum_refs, out_refs = split(
            refs, len(scalars) - 1, len(mine), len(theirs), 2, len(summand)
        )

        def store(i, tile, *values):
            for part, value in enumerate(values):
                if sum_refs:
                    value = value + rows_in(sum_refs, part, i, tile).astype(F32)
                for n in range(copies):
                    put_rows(out_refs[n * cuts : (n + 1) * cuts], part, i, tile, value)

        def work(n):
            held = number ^ n
            own = slice(held * half, (held + 1) * half)
            other = slice((1 - held) * half, (2 - held) * half)
            adjoint_into(mine_refs, theirs_refs, right_refs[n], own, other, own, store)

        def keep():
            tile = min(mine[0].shape[1], size // cuts)
            for i in range(0, size, tile):
                for part in range(2):
                    for n in range(copies):
                        value = rows_in(sum_refs, part, i, tile)
                        put_rows(out_refs[n * cuts : (n + 1) * cuts], part, i, tile, value)

        where_active(
            active_refs[0] if active_refs else None,
            lambda: either(core_ref, number, work),
            keep,
        )

    arrays = [*mine, *theirs, *rights, *summand]
    found = call(
        kernel,
        [block(2, size // cuts, half)] * (cuts * copies),
        scalars,
        arrays,
        16 * size * half * half,
        (),
        after,
    )
    if copies == 2:
        return found[:cuts], found[cuts:]
    return [found] if cuts == 1 else list(found)


def adjoint_own(core, mines, theirs, right, sums, other_sums):
    half, size = mines[0][0].shape[2], right.shape[1]
    lists = [*mines, *theirs, *sums, *other_sums]

    def kernel(core_ref, right_ref, *refs):
        *groups, (out_ref, held, sem) = split(refs, *(len(each) for each in lists))
        tile = min(256, mines[0][0].shape[1])

        def moved(i):
            at = slice(i, i + tile)
            return pltpu.make_async_copy(
                held.at[:, at, :], out_ref.at[:, at, :], sem.at[i // tile]
            )

        def work(n):
            mine_refs, theirs_refs, sum_refs, other_refs = groups[n::2]
            own, other = slice(n * half, (n + 1) * half), slice((1 - n) * half, (2 - n) * half)
            for i in range(0, size, tile):
                for to, summand in ((own, sum_refs), (other, other_refs)):

                    def store(i, tile, *values):
                        for part, value in enumerate(values):
                            value = value + rows_in(summand, part, i, tile).astype(F32)
                            held[part, i : i + tile, to] = value.astype(BF)

                    adjoint_into(mine_refs, theirs_refs, right_ref, own, other, to, store, (i, i + tile))
                moved(i).start()

        either(core_ref, 0, work)
        for i in range(0, size, tile):
            moved(i).wait()

    out = jax.ShapeDtypeStruct((2, size, size), BF)
    steps = size // min(256, mines[0][0].shape[1])
    scratch = [pltpu.VMEM(out.shape, BF), pltpu.SemaphoreType.DMA((steps,))]
    return call(
        kernel, [out], [core], [right, *sum(lists, [])], 8 * size**3, scratch, to_hbm=True
    )


def on_device(left_green, coupling, previous_lesser, screened, offsets, occupation):
    energies, slabs = lax.axis_size("energy"), lax.axis_size("slab")
    me, slab = lax.axis_index("energy"), lax.axis_index("slab")
    pairs = energies // 2
    pair, core = me // 2, me % 2
    first = core == 0
    size = coupling.shape[1]
    half = size // 2
    core_s = core[None]

    def swap(value):
        return lax.ppermute(value, "energy", [(i, i ^ 1) for i in range(energies)])

    def to_even(value):
        return lax.ppermute(value, "energy", [(i + 1, i) for i in range(0, energies, 2)])

    def to_odd(value):
        return lax.ppermute(value, "energy", [(i, i + 1) for i in range(0, energies, 2)])

    def by_energy(own, other):
        return jnp.where(first, own, other), jnp.where(first, other, own)

    green = left_green[:, 0, 0]
    before = previous_lesser[:, 0, 0]

    def column_half(value):
        return lax.dynamic_slice_in_dim(value, core * half, half, value.ndim - 1)

    both = [before, swap(before)]
    two = jnp.concatenate([offsets, swap(offsets)])
    spread = pairs in (2, 4) and size % (16 * pairs) == 0
    if spread:
        rows = size // pairs

        def across(value, d):
            moves = [(i, i ^ (2 * d)) for i in range(energies)]
            return lax.ppermute(value, "energy", moves)

        def patch(value, which):
            corner = (0, which * rows, core * half)
            return lax.dynamic_slice(value, corner, (2, rows, half))

        notes = jnp.pad(two.reshape(2 * MODES, 1).astype(BF), ((0, 16 - 2 * MODES), (0, 0)))
        notes = jnp.broadcast_to(notes, (16, half))
        order = list(reversed(range(1, pairs)))

        def patches(which):
            return jnp.concatenate(
                [patch(value, which).reshape(2 * rows, half) for value in both] + [notes]
            )

        sent = [patches(pair ^ d) for d in range(pairs)]
        pieces = sent[:1] + [None] * (pairs - 1)
        for d in order:
            pieces[d] = across(sent[d], d)
        first_sent = sent[1:]
        weights = patch(screened[:, 0], pair)
        places = pair ^ jnp.arange(pairs, dtype=jnp.int32)
        scalars = [me[None]]

        def spots(scalar_refs, carrier_refs):
            here = scalar_refs[0][0]
            found = [[None] * pairs for _ in range(2)]
            core_here = lax.rem(here, 2)
            for d in range(pairs):
                note = carrier_refs[d]
                line = lax.broadcasted_iota(jnp.int32, note.shape, 0)
                for n in range(2):
                    holder = here ^ (2 * d) ^ (core_here ^ n)
                    at = []
                    for m in range(MODES):
                        wanted_line = MODES * (core_here ^ n) + m
                        o = jnp.max(jnp.where(line == wanted_line, note, 0))
                        higher = lax.rem(holder + o, energies) ^ here
                        lower = lax.rem(holder - o + energies, energies) ^ here
                        at.append((higher, lower))
                    found[n][d] = at
            return found[0] + found[1]
    else:
        near = (REACH + 1) // 2
        pieces = []
        for d in range(-near, near + 1):
            moves = [(i, (i - 2 * d) % energies) for i in range(energies)]
            value = jnp.concatenate([column_half(v).reshape(2 * size, half) for v in both])
            pieces.append(lax.ppermute(value, "energy", moves) if d else value)
        weights = column_half(screened[:, 0])
        places, first_sent = None, []
        scalars = [core_s, two]

        def spots(scalar_refs, piece_refs):
            core_ref, two_ref = scalar_refs

            def place(away):
                away = away + 2 * near
                return 2 * lax.div(away, 2) + (lax.rem(away, 2) ^ core_ref[0])

            found = []
            for n in range(2):
                shift = [two_ref[core_ref[0] ^ n, m] for m in range(MODES)]
                found.append([(place(n + o), place(n - o)) for o in shift])
            return found

    own, own_sent = transfer_of(green, coupling[0], 2, first_sent)

    def maps_before(span, own):
        found, moving = [], own
        for hop in range(span):
            moves = [
                (s + hop - 1, s + hop)
                for s in range(3 * span, slabs, 2 * span)
                if s + hop < slabs
            ]
            moving = lax.ppermute(moving, "slab", moves)
            found.append(moving)
        return found

    def swap_all(values):
        return [swap(value) for value in values]

    def arrivals(span, values):
        groups = []
        for moving in values:
            group = []
            for hop in range(span):
                moves = [
                    (s + hop - 1, s + hop)
                    for s in range(span, slabs, 2 * span)
                    if s + hop < slabs
                ]
                moving = lax.ppermute(moving, "slab", moves)
                group.append(moving)
            groups.append(group)
        return groups

    other_green = swap(green)
    lefts = (green, other_green)
    above_by = weights.astype(F32)
    below_by = above_by * occupation[:, None, None]
    found = self_energy_patch(
        spots, scalars, above_by, below_by, pieces, 2 * pairs if spread else 2
    )
    maps = (own, transfer_of(other_green, coupling[0], 1, found[:1]))
    befores = maps_before(1, own_sent) if slabs > 2 else []
    if spread:
        early, late = list(found[:pairs]), list(found[pairs:])
        for d in order:
            early[d] = across(early[d], d)
        early = [[part] for part in early]
        *product, late[1], late[2:] = (
            lambda out: (*out[:CUTS], out[CUTS], list(out[CUTS + 1 :]))
        )(times(core_s, 0, lefts, early, places, maps[1:], late[1:]))
        for d in order:
            late[d] = across(late[d], d)
    else:
        product = times(core_s, 0, lefts, [[found[0]]], None, maps[1:])
        late = [found[1]]
    sums = [adjoint_half(core_s, 0, product, swap_all(product), lefts)]
    groups = [arrivals(1, sums[0])]
    product = times(core_s, 1, lefts, [[part] for part in late], places, sums[0])
    source, source_sent = adjoint_half(
        core_s, 1, product, swap_all(product), lefts, after=befores, copies=2
    )
    sums.append(source)
    groups.append(arrivals(1, source_sent))

    span = 1
    while 2 * span < slabs:
        active = lax.rem(slab // span, 2)[None]
        carried = times(core_s, 0, maps, groups[0], None, sums[1])
        early, early_sent = adjoint_half(
            core_s, 0, carried, swap_all(carried), maps, sums[0], PARTS, copies=2
        )
        early_groups = arrivals(2 * span, early_sent)
        own = composed(active, own, befores, after=early)
        ahead = [group[0] for group in early_groups]
        carried = times(core_s, 1, maps, groups[1], None, [own, *early, *ahead[:AHEAD]], active=active)
        behind = ahead[AHEAD:]
        late = adjoint_half(core_s, 1, carried, swap_all(carried), maps, sums[1], 2, behind, active=active)
        sums, groups = [early, late], [early_groups, arrivals(2 * span, late)]
        maps = (own, swap(own))
        span *= 2
        if 2 * span < slabs:
            befores = maps_before(span, own)
    if slabs > 1:
        others = [swap_all(value) for value in sums]
        carried = [times(core_s, 0, maps, groups[0])]
        theirs = [swap_all(carried[0])]
        carried.append(times(core_s, 1, maps, groups[1], None, theirs[0]))
        theirs.append(swap_all(carried[1]))
        result = adjoint_own(core_s, carried, theirs, maps[0], sums, others)
        return result[:, None, None]
    sums = [value[0] for value in sums]
    result = jnp.where(first, sums[0], sums[1])
    other = swap(jnp.where(first, sums[1], sums[0]))
    return jnp.concatenate(by_energy(result, other), axis=2)[:, None, None]


def solution(mesh):
    placed = (
        P(None, "energy", "slab", None, None),
        P("slab", None, None),
        P(None, "energy", "slab", None, None),
        P(None, "slab", None, None),
        P("energy", None),
        P(),
    )
    return jax.shard_map(
        on_device,
        mesh=mesh,
        in_specs=placed,
        out_specs=P(None, "energy", "slab", None, None),
        check_vma=False,
    )
```
